32 devices in a mesh: rows: 8 (over z, y), rhs: 4 (over x, core).
Axes of the slice: x: 2, y: 2, z: 4, core: 2. Of those that a mesh axis runs over, the one named last changes fastest.
Arguments:
- lower_panels: bfloat16 [32768, 1024], P('rows', 'rhs'), may hold values from -0.046875 to 0.046875
- parent_solution: bfloat16 [32768, 2048], P('rows', 'rhs'), may hold values from -6 to 6
- parent_rows: int32 [32768], P('rows'), may hold values from 0 to 32767, as said below
- live_counts: int32 [8], P('rows'), may hold values from 512 to 4096, as said below
- front_rhs: bfloat16 [1024, 2048], P('rows', 'rhs'), may hold values from -6 to 6
- coupling: float32 [512, 512], replicated, may hold values from -0.25 to 0.25
- inverse_one: float32 [512, 512], replicated, as said below
- inverse_two: float32 [512, 512], replicated, as said below
Outputs:
- solution: float32 [1024, 2048], P('rows', 'rhs')
The draws below stay inside these ranges and needn't reach their ends.
Inputs may be any that keep to these rules, and one draw needn't show every extreme that they name: `parent_rows`: the 128 entries of an aligned block of one device's 4096 entries all lie among the 4096 rows of one index of rows, the block's owner; two blocks of one device have the same owner exactly when their block numbers differ by a multiple of 8. `live_counts`: the live rows of an index are its first ones. Each count is 4096 divided by 1, 2, 4 or 8, and some index has all 4096. `inverse_one`: upper triangular. `inverse_two`: upper triangular.
All inputs are finite; a program needn't handle non-finite values.
Results may differ from the reference program's by a relative error of at most 0.0003.
Values may be sent and summed in bfloat16 or wider, within the bound.
No kernel may reach another device: no remote copies, remote signals or barrier semaphores. Data moves between devices by JAX's collectives and lax.ppermute only.
A program may use at most 64 MiB of HBM per device.

```python
import math
import jax
import jax.numpy as jnp
from jax import lax

PANEL = 512
R = 2048
BLK = 128
ROWS_DEV = 4096
ROWS = 32768
N_ROWS = 8


def draw_parent_rows(key, part):
    block_count = ROWS_DEV // BLK
    device_keys = jax.random.split(jax.random.fold_in(key, 11), N_ROWS)
    orders = jax.vmap(lambda one_key: jax.random.permutation(one_key, N_ROWS))(device_keys)
    owners = orders[:, jnp.arange(block_count) % N_ROWS]
    offsets = jax.random.randint(jax.random.fold_in(key, 12), (N_ROWS, block_count, BLK), 0, ROWS_DEV)
    chosen = owners[:, :, None] * ROWS_DEV + offsets
    return chosen.reshape(ROWS).astype(jnp.int32)


def draw_live_counts(key, part):
    shifts = jax.random.randint(jax.random.fold_in(key, 21), (N_ROWS,), 0, 4)
    fullest = jax.random.randint(jax.random.fold_in(key, 22), (), 0, N_ROWS)
    shifts = jnp.where(jnp.arange(N_ROWS) == fullest, 0, shifts)
    return jnp.right_shift(jnp.full((N_ROWS,), ROWS_DEV, jnp.int32), shifts.astype(jnp.int32)).astype(jnp.int32)


def triangle(key):
    diag_key, off_key = jax.random.split(key, 2)
    diagonal = jax.random.uniform(diag_key, (PANEL,), jnp.float32, 0.5, 1.5)
    offdiag = jax.random.normal(off_key, (PANEL, PANEL), jnp.float32) * (0.6 / math.sqrt(PANEL))
    matrix = jnp.triu(offdiag, 1) + jnp.diag(diagonal)
    return matrix


def draw_inverse_one(key, part):
    return triangle(jax.random.fold_in(key, 31))


def draw_inverse_two(key, part):
    return triangle(jax.random.fold_in(key, 32))


def spiked(array, stream_key, source, target, parts, factor):
    def block_of(dim):
        return (jnp.arange(array.shape[dim]) // (array.shape[dim] // parts)).reshape((-1,) + (1,) * (array.ndim - 1 - dim))

    one_side = jax.random.permutation(stream_key, parts)[block_of(target)]
    other_side = (block_of(target) + parts // 2) % parts
    return jnp.where((block_of(source) == one_side) | (block_of(source) == other_side), factor * array, array)


def shard_levels(rng, shape, cuts, smallest, high):
    loudness = 1.0
    for axis_at, blocks in cuts:
        steps = jax.random.uniform(jax.random.fold_in(jax.random.fold_in(rng, 6), axis_at), (blocks,), jnp.float32, smallest / len(cuts), high / len(cuts))
        loudness = loudness * jnp.repeat(jnp.exp(steps), shape[axis_at] // blocks).reshape((-1,) + (1,) * (len(shape) - 1 - axis_at))
    return loudness


def normal_values(own_key, dims, spread, limit, shards=(), kind=jnp.bfloat16):
    result = jax.random.normal(own_key, dims, jnp.float32) * spread
    if len(shards) > 0:
        result = shard_levels(own_key, dims, shards, -0.22, 0.18) * result
    return jnp.clip(result, min=-limit, max=limit).astype(kind)


def heavy_noise(key, dims, spread, most, shards, heavy, held_as=jnp.bfloat16):
    values = spread * jax.random.normal(key, dims, jnp.float32)
    if shards:
        values = values * shard_levels(key, dims, shards, -0.22, 0.18)
    return jnp.clip(spiked(values, jax.random.fold_in(key, 3), *heavy), -most, most).astype(held_as)


def setup_inputs(seed: int = 0) -> dict:
    splits = jax.random.split(jax.random.key(seed), 9)
    return {
        "lower_panels": heavy_noise(splits[0], (ROWS, 2 * PANEL), ROWS ** -0.5, 0.046875, ((0, 8), (1, 4)), (0, 1, 8, 2.0)),
        "parent_solution": normal_values(splits[1], (ROWS, R), 1.0, 6.0, ((0, 8), (1, 4))),
        "parent_rows": draw_parent_rows(jax.random.fold_in(splits[8], 71), 0),
        "live_counts": draw_live_counts(jax.random.fold_in(splits[8], 71), 0),
        "front_rhs": normal_values(splits[4], (2 * PANEL, R), 1.0, 6.0, ((0, 8), (1, 4))),
        "coupling": normal_values(splits[5], (PANEL, PANEL), PANEL ** -0.5, 0.25, (), jnp.float32),
        "inverse_one": draw_inverse_one(jax.random.fold_in(splits[8], 71), 0),
        "inverse_two": draw_inverse_two(jax.random.fold_in(splits[8], 71), 0),
    }


def reference(lower_panels, parent_solution, parent_rows, live_counts, front_rhs, coupling, inverse_one, inverse_two):
    row_lists = parent_rows.reshape(N_ROWS, ROWS_DEV)
    positions = jnp.arange(ROWS_DEV, dtype=jnp.int32)

    def add_block(total, inputs):
        device, chosen, count = inputs
        fetched = parent_solution[chosen]
        fetched = jnp.where((positions < count)[:, None], fetched, jnp.zeros((), fetched.dtype))
        panel = lax.dynamic_slice_in_dim(lower_panels, (device * ROWS_DEV).astype(jnp.int32), ROWS_DEV, 0)
        term = jnp.dot(panel.T.astype(jnp.float32), fetched.astype(jnp.float32), precision=lax.Precision.HIGHEST)
        return total + term, None

    start_total = jnp.zeros((2 * PANEL, R), jnp.float32)
    total, _ = lax.scan(add_block, start_total, (jnp.arange(N_ROWS, dtype=jnp.int32), row_lists, live_counts))
    residual = front_rhs.astype(jnp.float32) - total
    second = jnp.dot(inverse_two, residual[PANEL:], precision=lax.Precision.HIGHEST)
    reduced = residual[:PANEL] - jnp.dot(coupling, second, precision=lax.Precision.HIGHEST)
    first = jnp.dot(inverse_one, reduced, precision=lax.Precision.HIGHEST)
    return jnp.concatenate([first, second], axis=0)
```

```python
import jax
import jax.numpy as jnp
from jax import lax
from jax.sharding import PartitionSpec as P

BLK = 128


def swap(array, axis, mask):
    size = lax.axis_size(axis)
    return lax.ppermute(array, axis, [(i, i ^ mask) for i in range(size)])


def full_dot(left, right):
    return jnp.dot(
        left, right, precision=lax.Precision.HIGHEST, preferred_element_type=jnp.float32
    )


def panel_dot(panel, rows):
    return lax.dot_general(
        panel, rows, (((0,), (0,)), ((), ())), preferred_element_type=jnp.float32
    )


def halving_sum(parts, order):
    for mask in order:
        keep = [r for r in parts if not r & mask]
        sent = jnp.stack([parts[r | mask] for r in keep])
        came = swap(sent, "rows", mask)
        parts = {r: parts[r] + came[i] for i, r in enumerate(keep)}
    return parts[0]


def body(
    lower_panels,
    parent_solution,
    parent_rows,
    live_counts,
    front_rhs,
    coupling,
    inverse_one,
    inverse_two,
):
    groups = lax.axis_size("rows")
    shares = lax.axis_size("rhs")
    me = lax.axis_index("rows")
    share = lax.axis_index("rhs")
    rows_dev = parent_rows.shape[0]
    slots = rows_dev // BLK // groups
    width = lower_panels.shape[1]
    columns = parent_solution.shape[1]
    panel = inverse_one.shape[0]
    pivot_share = front_rhs.shape[0]

    lists = parent_rows.reshape(slots, groups, BLK)
    owners = lists[0, :, 0] // rows_dev
    local = lists - (owners * rows_dev)[None, :, None]
    places = jnp.arange(groups, dtype=jnp.int32)
    blocks = lower_panels.reshape(slots, groups, BLK, width)
    live = (jnp.arange(rows_dev, dtype=jnp.int32) < live_counts[0]).reshape(slots, groups, BLK)

    def for_owner(mask):
        place = jnp.sum(jnp.where(owners == me ^ mask, places, 0))
        take = lambda a: lax.dynamic_index_in_dim(a, place, 1, keepdims=False)
        chunk = jnp.where(take(live)[..., None], take(blocks), jnp.zeros((), blocks.dtype))
        return chunk.reshape(slots * BLK, width), take(local)

    sends = [for_owner(mask) for mask in range(groups)]
    asked = [sends[0][1]] + [swap(sends[mask][1], "rows", mask) for mask in range(1, groups)]

    half = groups // 2
    chunks = {0: sends[0][0]}
    last = None
    for mask in list(range(half, groups)):
        sent = sends[mask][0]
        if last is not None:
            sent, last = lax.optimization_barrier((sent, last))
        chunks[mask] = last = swap(sent, "rows", mask)
    for mask in range(1, half):
        chunks[mask] = swap(sends[mask][0], "rows", mask)

    total = 0.0
    for mask in [0] + list(range(1, half)) + list(range(half, groups)):
        chunk = chunks[mask]
        near = jnp.concatenate(
            [chunk] + [swap(chunk, "rhs", other) for other in range(2, shares, 2)], axis=1
        )
        far = swap(near, "rhs", 1)
        picked = parent_solution[asked[mask].reshape(-1)]
        total = total + panel_dot(jnp.concatenate([near, far], axis=1), picked)

    shape = (shares, width, columns)
    order = jnp.arange(shares, dtype=jnp.int32) ^ share
    position = (order & 1) * (shares // 2) + (order >> 1)
    product = total.reshape(shape)[position].reshape(2 * panel, columns)
    placed = lax.dynamic_update_slice(
        jnp.zeros((2 * panel, columns), jnp.float32), front_rhs.astype(jnp.float32), (me * pivot_share, 0)
    )
    resid = placed - product

    outs = []
    middle = columns // 2
    bits = [1 << b for b in range(groups.bit_length() - 1)]
    for at, order in ((0, bits), (middle, bits[1:] + bits[:1])):
        part = resid[:, at : at + middle]
        second = full_dot(inverse_two, part[panel:])
        first = full_dot(inverse_one, part[:panel] - full_dot(coupling, second))
        solved = jnp.concatenate([first, second], axis=0).reshape(groups, pivot_share, middle)
        parts = {
            r: lax.dynamic_index_in_dim(solved, me ^ r, 0, keepdims=False) for r in range(groups)
        }
        outs.append(halving_sum(parts, order))
    return jnp.concatenate(outs, axis=1)


def solution(mesh):
    return jax.shard_map(
        body,
        mesh=mesh,
        in_specs=(
            P("rows", "rhs"),
            P("rows", "rhs"),
            P("rows"),
            P("rows"),
            P("rows", "rhs"),
            P(),
            P(),
            P(),
        ),
        out_specs=P("rows", "rhs"),
        check_vma=False,
    )
```

```python
import functools

import jax
import jax.numpy as jnp
from jax import lax
from jax.experimental import pallas as pl
from jax.experimental.pallas import tpu as pltpu
from jax.sharding import PartitionSpec as P

BLK = 128
LANES = 128
ANY = pl.BlockSpec(memory_space=pl.ANY)
VMEM = pl.BlockSpec(memory_space=pltpu.VMEM)
SMEM = pl.BlockSpec(memory_space=pltpu.SMEM)


def swap(array, axis, mask):
    size = lax.axis_size(axis)
    return lax.ppermute(array, axis, [(i, i ^ mask) for i in range(size)])


def pack_kernel(groups, slots, rows_ref, live_ref, lists_ref, panels_ref, *refs):
    chunks, place_ref, tile_ref = refs[: groups + 1], refs[groups + 1], refs[groups + 2]
    me = lax.axis_index("rows")
    rows_dev = rows_ref.shape[0]
    for place in range(groups):
        place_ref[lax.div(rows_ref[place * BLK], rows_dev) ^ me] = place
    live_blocks = lax.div(live_ref[0], BLK)
    tile_ref[...] = jnp.zeros_like(tile_ref)
    for mask in range(groups):
        start = (mask ^ me) * rows_dev
        for slot in range(slots):
            row = slot * groups + place_ref[mask]
            local = lists_ref[pl.ds(row, 1), :] - start
            tile_ref[pl.ds(2 * slot, 1), pl.ds(0, BLK)] = (local >> 8).astype(jnp.float32)
            tile_ref[pl.ds(2 * slot + 1, 1), pl.ds(0, BLK)] = (local & 255).astype(jnp.float32)
        chunk = chunks[mask]
        tile = tile_ref.shape[0]
        chunk[pl.ds(chunk.shape[0] - tile, tile), :] = tile_ref[...].astype(chunk.dtype)
        for at, count, part, into in pieces_of(mask, groups, slots):
            ref = chunks[mask + part]
            block = at // BLK * groups + place_ref[mask]

            @pl.when(block < live_blocks)
            def _():
                first = pl.multiple_of(block * BLK + at % BLK, 16)
                ref[pl.ds(into, count), :] = panels_ref[pl.ds(first, count), :]

            @pl.when(block >= live_blocks)
            def _():
                ref[pl.ds(into, count), :] = jnp.zeros((count, ref.shape[1]), ref.dtype)


def pieces_of(mask, groups, slots):
    cut = slots * BLK // 2 if mask == groups - 1 else slots * BLK
    step = min(BLK, cut)
    for at in range(0, slots * BLK, step):
        yield at, step, int(at >= cut), at % cut


def list_rows(slots):
    return -(-2 * slots // 16) * 16


def pack(lower_panels, parent_rows, live_counts, groups, slots):
    rows_dev, width = lower_panels.shape
    rows, extra = slots * BLK, list_rows(slots)
    counts = [rows + extra] * (groups - 1) + [rows // 2 + extra, rows // 2]
    return pl.pallas_call(
        functools.partial(pack_kernel, groups, slots),
        out_shape=[jax.ShapeDtypeStruct((n, width), lower_panels.dtype) for n in counts],
        in_specs=[SMEM, SMEM, VMEM, VMEM],
        out_specs=[VMEM] * len(counts),
        scratch_shapes=[
            pltpu.SMEM((groups,), jnp.int32),
            pltpu.VMEM((extra, width), jnp.float32),
        ],
        compiler_params=pltpu.CompilerParams(vmem_limit_bytes=24 * 2**20),
        name="pack",
    )(parent_rows, live_counts, parent_rows.reshape(rows_dev // BLK, BLK), lower_panels)


def pick_kernel(groups, slots, parent_ref, *refs):
    chunks, (out_ref, wide, stage, tiles_ref, lists_ref, rows_ref, sems) = refs[:groups], refs[groups:]
    extra = list_rows(slots)
    reads = []
    for mask, chunk in enumerate(chunks):
        from_ref = chunk.at[pl.ds(chunk.shape[0] - extra, extra), :]
        reads.append(pltpu.make_async_copy(from_ref, tiles_ref.at[mask], sems.at[mask]))
        reads[-1].start()
    for read in reads:
        read.wait()
    rows, columns = parent_ref.shape
    tiles = columns // LANES
    for mask in range(groups):
        for slot in range(slots):
            pair = tiles_ref[mask, :, pl.ds(0, BLK)].astype(jnp.float32)[2 * slot : 2 * slot + 2]
            local = pair[0:1] * 256.0 + pair[1:2]
            lists_ref[pl.ds(mask * slots + slot, 1), :] = local.astype(jnp.int32) * tiles
    move = pltpu.make_async_copy(lists_ref, rows_ref, sems.at[groups])
    move.start()
    step = min(rows, 256)

    @pl.loop(0, rows // step)
    def _(i):
        at = pl.multiple_of(i * step, step)
        for tile in range(tiles):
            wide[pl.ds(at * tiles + tile, step, stride=tiles), :] = parent_ref[
                pl.ds(at, step), pl.ds(tile * LANES, LANES)
            ].astype(jnp.float32)

    move.wait()
    nothing = jnp.zeros((extra, columns), out_ref.dtype)
    count = slots * BLK

    @pl.loop(0, groups)
    def _(mask):
        @pl.loop(0, slots)
        def _(slot):
            base = slot * (BLK * tiles)
            for i in range(BLK):
                row = pl.multiple_of(rows_ref[mask * slots + slot, i], tiles)
                into = pl.multiple_of(base + i * tiles, tiles)
                stage[pl.ds(into, tiles), :] = wide[pl.ds(row, tiles), :]

        def write(into, first, rows):
            for tile in range(tiles):
                out_ref[pl.ds(into, rows), pl.ds(tile * LANES, LANES)] = stage[
                    pl.ds(first * tiles + tile, rows, stride=tiles), :
                ].astype(out_ref.dtype)

        into = pl.multiple_of(mask * (count + extra), 16)

        @pl.when(mask < groups - 1)
        def _():
            write(into, 0, count)
            out_ref[pl.ds(pl.multiple_of(into + count, 16), extra), :] = nothing

        @pl.when(mask == groups - 1)
        def _():
            last, cut = (groups - 1) * (count + extra), count // 2
            write(last, 0, cut)
            out_ref[pl.ds(last + cut, extra), :] = nothing
            write(last + cut + extra, cut, cut)


def pick(parent, chunks, slots):
    groups = len(chunks)
    columns = parent.shape[1]
    tiles = columns // LANES
    extra = list_rows(slots)
    width = chunks[0].shape[1]
    return pl.pallas_call(
        functools.partial(pick_kernel, groups, slots),
        out_shape=jax.ShapeDtypeStruct((groups * (slots * BLK + extra), columns), parent.dtype),
        in_specs=[VMEM] + [ANY] * groups,
        out_specs=VMEM,
        scratch_shapes=[
            pltpu.VMEM((parent.shape[0] * tiles, LANES), jnp.float32),
            pltpu.VMEM((slots * BLK * tiles, LANES), jnp.float32),
            pltpu.VMEM((groups, extra, width), parent.dtype),
            pltpu.VMEM((groups * slots, BLK), jnp.int32),
            pltpu.SMEM((groups * slots, BLK), jnp.int32),
            pltpu.SemaphoreType.DMA((groups + 1,)),
        ],
        compiler_params=pltpu.CompilerParams(vmem_limit_bytes=48 * 2**20),
        name="pick",
    )(parent, *chunks)


def split(value):
    high = value.astype(jnp.bfloat16)
    return high, (value - high.astype(jnp.float32)).astype(jnp.bfloat16)


def dot3(left, right):
    dot = functools.partial(jnp.dot, preferred_element_type=jnp.float32)
    (lh, ll), (rh, rl) = left, right
    return dot(lh, rh) + (dot(lh, rl) + dot(ll, rh))


def solve_kernel(orders, near_ref, far_ref, front_ref, coup_ref, one_ref, two_ref, *refs):
    outs, resid = refs[:4], refs[4]
    me = lax.axis_index("rows")
    share = lax.axis_index("rhs")
    pivot_share = front_ref.shape[0]
    pivots, columns = resid.shape
    panel = pivots // 2
    half_shares = lax.axis_size("rhs") // 2
    width = near_ref.shape[0] // half_shares
    for odd, part_ref in ((0, near_ref), (1, far_ref)):
        for i in range(half_shares):
            at = pl.multiple_of((share ^ (2 * i + odd)) * width, width)
            resid[pl.ds(at, width), :] = -part_ref[pl.ds(i * width, width), :]
    mine = pl.ds(pl.multiple_of(me * pivot_share, pivot_share), pivot_share)
    resid[mine, :] += front_ref[...].astype(jnp.float32)
    two, one, coup = split(two_ref[...]), split(one_ref[...]), split(coup_ref[...])
    middle = columns // 2
    groups = pivots // pivot_share
    for side in range(2):
        cols = pl.ds(side * middle, middle)
        second = dot3(two, split(resid[pl.ds(panel, panel), cols]))
        reduced = resid[pl.ds(0, panel), cols] - dot3(coup, split(second))
        first = dot3(one, split(reduced))
        keep_ref, send_ref = outs[2 * side : 2 * side + 2]
        order = orders[side]
        for block in range(groups):
            source = first if block < groups // 2 else second
            at = (block % (groups // 2)) * pivot_share
            value = source[at : at + pivot_share, :]
            rel = block ^ me
            place = sum(
                ((rel >> bit) & 1) << (len(order) - 1 - i) for i, bit in enumerate(order) if i
            )
            sent = (rel >> order[0]) & 1

            @pl.when(sent == 0)
            def _():
                keep_ref[place] = value

            @pl.when(sent == 1)
            def _():
                send_ref[place] = value


def solve(orders, near, far, front_rhs, coupling, one, two, groups):
    pivot_share, columns = front_rhs.shape
    pivots = groups * pivot_share
    out = jax.ShapeDtypeStruct((groups // 2, pivot_share, columns // 2), jnp.float32)
    return pl.pallas_call(
        functools.partial(solve_kernel, orders),
        out_shape=[out] * 4,
        in_specs=[VMEM] * 6,
        out_specs=[VMEM] * 4,
        scratch_shapes=[pltpu.VMEM((pivots, columns), jnp.float32)],
        compiler_params=pltpu.CompilerParams(vmem_limit_bytes=48 * 2**20),
        name="solve",
    )(near, far, front_rhs, coupling, one, two)


def panel_dot(panel, rows):
    return lax.dot_general(
        panel, rows, (((0,), (0,)), ((), ())), preferred_element_type=jnp.float32
    )


def body(
    lower_panels,
    parent_solution,
    parent_rows,
    live_counts,
    front_rhs,
    coupling,
    inverse_one,
    inverse_two,
):
    groups = lax.axis_size("rows")
    shares = lax.axis_size("rhs")
    rows_dev = parent_rows.shape[0]
    slots = rows_dev // BLK // groups
    chunk_rows = slots * BLK
    bits = list(range(groups.bit_length() - 1))

    chunks = pack(lower_panels, parent_rows, live_counts, groups, slots)
    half = groups // 2
    mask_of = list(range(groups)) + [groups - 1]
    got, nears, fars = {0: chunks[0]}, {}, {}

    def after(value, *events):
        held = [store[key] for store, key in events]
        value, held = lax.optimization_barrier((value, held))
        for (store, key), now in zip(events, held):
            store[key] = now
        return value

    def move(at, *events):
        got[at] = swap(after(chunks[at], *events), "rows", mask_of[at])

    def cross(at, *events):
        own = after(got[at], *events)
        nears[at] = jnp.concatenate(
            [own] + [swap(own, "rhs", other) for other in range(2, shares, 2)], axis=1
        )

    runs = [[0], list(range(1, half)), [half, half + 1]] + [[at] for at in range(half + 2, groups + 1)]
    for at in range(half, groups + 1):
        move(at, *([(got, at - 2)] if at >= half + 2 else []))
    for at in range(1, half):
        move(at, *([(got, at - 9)] if at > 9 else []))
    starts = [0]
    for at in range(groups):
        starts.append(starts[at] + chunks[at].shape[0])
    def cross(own):
        return jnp.concatenate(
            [own] + [swap(own, "rhs", other) for other in range(2, shares, 2)], axis=1
        )
    near_total = far_total = 0.0
    picked = pick(parent_solution, [got[at] for at in range(groups)], slots)
    def add(i):
        rows = [picked[starts[at] : starts[at] + chunks[at].shape[0]] for at in runs[i]]
        rows = jnp.concatenate(rows, axis=0)
        return near_total + panel_dot(nears[i], rows), far_total + panel_dot(fars[i], rows)
    done = 0
    for r, run in enumerate(runs):
        if r == len(runs) - 1:
            while done < len(runs) - 1 - 2:
                near_total, far_total = add(done)
                done += 1
            got[groups], near_total, far_total = lax.optimization_barrier((got[groups], near_total, far_total))
        nears[r] = cross(jnp.concatenate([got[at] for at in run], axis=0))
        fars[r] = swap(nears[r], "rhs", 1)
    while done < len(runs):
        near_total, far_total = add(done)
        done += 1

    orders = (bits, bits[1:] + bits[:1])
    keep_a, send_a, keep_b, send_b = solve(
        orders, near_total, far_total, front_rhs, coupling, inverse_one, inverse_two, groups
    )
    for step in range(len(bits)):
        came_a = swap(send_a, "rows", 1 << orders[0][step])
        came_b = swap(send_b, "rows", 1 << orders[1][step])
        came_a, came_b = lax.optimization_barrier((came_a, came_b))
        middle = keep_a.shape[0] // 2
        send_a, send_b = keep_a[middle:] + came_a[middle:], keep_b[middle:] + came_b[middle:]
        if middle:
            keep_a, keep_b = keep_a[:middle] + came_a[:middle], keep_b[:middle] + came_b[:middle]
    return jnp.concatenate([send_a[0], send_b[0]], axis=1)


def solution(mesh):
    return jax.shard_map(
        body,
        mesh=mesh,
        in_specs=(
            P("rows", "rhs"),
            P("rows", "rhs"),
            P("rows"),
            P("rows"),
            P("rows", "rhs"),
            P(),
            P(),
            P(),
        ),
        out_specs=P("rows", "rhs"),
        check_vma=False,
    )
```

```python
import functools

import jax
import jax.numpy as jnp
from jax import lax
from jax.experimental import pallas as pl
from jax.experimental.pallas import tpu as pltpu
from jax.sharding import PartitionSpec as P

BLK = 128
LANES = 128
CODE_BITS = 14.96
ANY = pl.BlockSpec(memory_space=pl.ANY)
VMEM = pl.BlockSpec(memory_space=pltpu.VMEM)
SMEM = pl.BlockSpec(memory_space=pltpu.SMEM)


def swap(array, axis, mask):
    size = lax.axis_size(axis)
    return lax.ppermute(array, axis, [(i, i ^ mask) for i in range(size)])


def pack_kernel(groups, slots, rows_ref, live_ref, lists_ref, panels_ref, *refs):
    chunks, place_ref, tile_ref = refs[: groups + 1], refs[groups + 1], refs[groups + 2]
    me = lax.axis_index("rows")
    rows_dev = rows_ref.shape[0]
    for place in range(groups):
        place_ref[lax.div(rows_ref[place * BLK], rows_dev) ^ me] = place
    live_blocks = lax.div(live_ref[0], BLK)
    tile_ref[...] = jnp.zeros_like(tile_ref)
    for mask in range(groups):
        start = (mask ^ me) * rows_dev
        for slot in range(slots):
            row = slot * groups + place_ref[mask]
            local = lists_ref[pl.ds(row, 1), :] - start
            tile_ref[pl.ds(2 * slot, 1), pl.ds(0, BLK)] = (local >> 8).astype(jnp.float32)
            tile_ref[pl.ds(2 * slot + 1, 1), pl.ds(0, BLK)] = (local & 255).astype(jnp.float32)
        chunk = chunks[mask]
        tile = tile_ref.shape[0]
        chunk[pl.ds(chunk.shape[0] - tile, tile), :] = tile_ref[...].astype(chunk.dtype)
        for at, count, part, into in pieces_of(mask, groups, slots):
            ref = chunks[mask + part]
            block = at // BLK * groups + place_ref[mask]

            @pl.when(block < live_blocks)
            def _():
                first = pl.multiple_of(block * BLK + at % BLK, 16)
                ref[pl.ds(into, count), :] = panels_ref[pl.ds(first, count), :]

            @pl.when(block >= live_blocks)
            def _():
                ref[pl.ds(into, count), :] = jnp.zeros((count, ref.shape[1]), ref.dtype)


def pieces_of(mask, groups, slots):
    cut = slots * BLK // 2 if mask == groups - 1 else slots * BLK
    step = min(BLK, cut)
    for at in range(0, slots * BLK, step):
        yield at, step, int(at >= cut), at % cut


def list_rows(slots):
    return -(-2 * slots // 16) * 16


def pack(lower_panels, parent_rows, live_counts, groups, slots):
    rows_dev, width = lower_panels.shape
    rows, extra = slots * BLK, list_rows(slots)
    counts = [rows + extra] * (groups - 1) + [rows // 2 + extra, rows // 2]
    return pl.pallas_call(
        functools.partial(pack_kernel, groups, slots),
        out_shape=[jax.ShapeDtypeStruct((n, width), lower_panels.dtype) for n in counts],
        in_specs=[SMEM, SMEM, VMEM, VMEM],
        out_specs=[VMEM] * len(counts),
        scratch_shapes=[
            pltpu.SMEM((groups,), jnp.int32),
            pltpu.VMEM((extra, width), jnp.float32),
        ],
        compiler_params=pltpu.CompilerParams(vmem_limit_bytes=24 * 2**20),
        name="pack",
    )(parent_rows, live_counts, parent_rows.reshape(rows_dev // BLK, BLK), lower_panels)


def pick_kernel(groups, slots, parent_ref, *refs):
    chunks, (out_ref, wide, stage, tiles_ref, lists_ref, rows_ref, sems) = refs[:groups], refs[groups:]
    extra = list_rows(slots)
    reads = []
    for mask, chunk in enumerate(chunks):
        from_ref = chunk.at[pl.ds(chunk.shape[0] - extra, extra), :]
        reads.append(pltpu.make_async_copy(from_ref, tiles_ref.at[mask], sems.at[mask]))
        reads[-1].start()
    for read in reads:
        read.wait()
    rows, columns = parent_ref.shape
    tiles = columns // LANES
    for mask in range(groups):
        for slot in range(slots):
            pair = tiles_ref[mask, :, pl.ds(0, BLK)].astype(jnp.float32)[2 * slot : 2 * slot + 2]
            local = pair[0:1] * 256.0 + pair[1:2]
            lists_ref[pl.ds(mask * slots + slot, 1), :] = local.astype(jnp.int32) * tiles
    move = pltpu.make_async_copy(lists_ref, rows_ref, sems.at[groups])
    move.start()
    step = min(rows, 256)

    @pl.loop(0, rows // step)
    def _(i):
        at = pl.multiple_of(i * step, step)
        for tile in range(tiles):
            wide[pl.ds(at * tiles + tile, step, stride=tiles), :] = parent_ref[
                pl.ds(at, step), pl.ds(tile * LANES, LANES)
            ].astype(jnp.float32)

    move.wait()
    nothing = jnp.zeros((extra, columns), out_ref.dtype)
    count = slots * BLK

    @pl.loop(0, groups)
    def _(mask):
        @pl.loop(0, slots)
        def _(slot):
            base = slot * (BLK * tiles)
            for i in range(BLK):
                row = pl.multiple_of(rows_ref[mask * slots + slot, i], tiles)
                into = pl.multiple_of(base + i * tiles, tiles)
                stage[pl.ds(into, tiles), :] = wide[pl.ds(row, tiles), :]

        def write(into, first, rows):
            for tile in range(tiles):
                out_ref[pl.ds(into, rows), pl.ds(tile * LANES, LANES)] = stage[
                    pl.ds(first * tiles + tile, rows, stride=tiles), :
                ].astype(out_ref.dtype)

        into = pl.multiple_of(mask * (count + extra), 16)

        @pl.when(mask < groups - 1)
        def _():
            write(into, 0, count)
            out_ref[pl.ds(pl.multiple_of(into + count, 16), extra), :] = nothing

        @pl.when(mask == groups - 1)
        def _():
            last, cut = (groups - 1) * (count + extra), count // 2
            write(last, 0, cut)
            out_ref[pl.ds(last + cut, extra), :] = nothing
            write(last + cut + extra, cut, cut)


def pick(parent, chunks, slots):
    groups = len(chunks)
    columns = parent.shape[1]
    tiles = columns // LANES
    extra = list_rows(slots)
    width = chunks[0].shape[1]
    return pl.pallas_call(
        functools.partial(pick_kernel, groups, slots),
        out_shape=jax.ShapeDtypeStruct((groups * (slots * BLK + extra), columns), parent.dtype),
        in_specs=[VMEM] + [ANY] * groups,
        out_specs=VMEM,
        scratch_shapes=[
            pltpu.VMEM((parent.shape[0] * tiles, LANES), jnp.float32),
            pltpu.VMEM((slots * BLK * tiles, LANES), jnp.float32),
            pltpu.VMEM((groups, extra, width), parent.dtype),
            pltpu.VMEM((groups * slots, BLK), jnp.int32),
            pltpu.SMEM((groups * slots, BLK), jnp.int32),
            pltpu.SemaphoreType.DMA((groups + 1,)),
        ],
        compiler_params=pltpu.CompilerParams(vmem_limit_bytes=48 * 2**20),
        name="pick",
    )(parent, *chunks)


def split(value):
    high = value.astype(jnp.bfloat16)
    return high, (value - high.astype(jnp.float32)).astype(jnp.bfloat16)


def dot3(left, right):
    dot = functools.partial(jnp.dot, preferred_element_type=jnp.float32)
    (lh, ll), (rh, rl) = left, right
    return dot(lh, rh) + (dot(lh, rl) + dot(ll, rh))


def encode(value):
    value = value * 0.25
    most = jnp.maximum(jnp.max(jnp.abs(value), axis=0, keepdims=True), 1e-30)
    exponent = jnp.floor(8.0 * jnp.log2(most)) + 1.0
    codes = jnp.round(value * jnp.exp2(CODE_BITS - 0.125 * exponent))
    return codes.astype(jnp.int32).astype(jnp.int16), exponent


def decode(codes, exponent):
    scale = jnp.exp2(0.125 * exponent - CODE_BITS)
    return codes.astype(jnp.int32).astype(jnp.float32) * scale * 4.0


def scale_rows(blocks):
    return -(-blocks // 16) * 16


def write_message(message_ref, scales_ref, blocks):
    count, rows, _ = blocks.shape
    scales_ref[...] = jnp.zeros_like(scales_ref)
    for i in range(count):
        codes, exponent = encode(blocks[i])
        message_ref[pl.ds(i * rows, rows), :] = codes
        scales_ref[pl.ds(i, 1), :] = exponent
    message_ref[pl.ds(count * rows, scales_ref.shape[0]), :] = (
        scales_ref[...].astype(jnp.int32).astype(jnp.int16)
    )


def read_message(message_ref, rows, wanted):
    count = message_ref.shape[0] // rows
    tail = message_ref[pl.ds(count * rows, message_ref.shape[0] - count * rows), :]
    exponents = tail.astype(jnp.int32).astype(jnp.float32)
    return [decode(message_ref[pl.ds(i * rows, rows), :], exponents[i : i + 1]) for i in wanted]


def message_shape(blocks, rows, columns):
    return jax.ShapeDtypeStruct((blocks * rows + scale_rows(blocks), columns), jnp.int16)


def solve_kernel(side, order, near_ref, far_ref, front_ref, coup_ref, one_ref, two_ref, *refs):
    keep_ref, message_ref, resid, send_ref, scales_ref = refs
    me = lax.axis_index("rows")
    share = lax.axis_index("rhs")
    pivot_share = front_ref.shape[0]
    pivots, columns = resid.shape
    panel = pivots // 2
    half_shares = lax.axis_size("rhs") // 2
    width = near_ref.shape[0] // half_shares
    groups = pivots // pivot_share
    cols = pl.ds(side * columns, columns)
    for odd, part_ref in ((0, near_ref), (1, far_ref)):
        for i in range(half_shares):
            at = pl.multiple_of((share ^ (2 * i + odd)) * width, width)
            resid[pl.ds(at, width), :] = -part_ref[pl.ds(i * width, width), cols]
    mine = pl.ds(pl.multiple_of(me * pivot_share, pivot_share), pivot_share)
    resid[mine, :] += front_ref[:, cols].astype(jnp.float32)
    second = dot3(split(two_ref[...]), split(resid[pl.ds(panel, panel), :]))
    reduced = resid[pl.ds(0, panel), :] - dot3(split(coup_ref[...]), split(second))
    first = dot3(split(one_ref[...]), split(reduced))
    for block in range(groups):
        source = first if block < groups // 2 else second
        at = (block % (groups // 2)) * pivot_share
        value = source[at : at + pivot_share, :]
        rel = block ^ me
        place = sum(
            ((rel >> bit) & 1) << (len(order) - 1 - i) for i, bit in enumerate(order) if i
        )
        sent = (rel >> order[0]) & 1

        @pl.when(sent == 0)
        def _():
            keep_ref[place] = value

        @pl.when(sent == 1)
        def _():
            send_ref[place] = value

    write_message(message_ref, scales_ref, send_ref)


def solve(side, order, near, far, front_rhs, coupling, one, two, groups):
    pivot_share, columns = front_rhs.shape
    pivots, columns, half = groups * pivot_share, columns // 2, groups // 2
    blocks = jax.ShapeDtypeStruct((half, pivot_share, columns), jnp.float32)
    return pl.pallas_call(
        functools.partial(solve_kernel, side, order),
        out_shape=[blocks, message_shape(half, pivot_share, columns)],
        in_specs=[VMEM] * 6,
        out_specs=[VMEM] * 2,
        scratch_shapes=[
            pltpu.VMEM((pivots, columns), jnp.float32),
            pltpu.VMEM(blocks.shape, jnp.float32),
            pltpu.VMEM((scale_rows(half), columns), jnp.float32),
        ],
        compiler_params=pltpu.CompilerParams(vmem_limit_bytes=48 * 2**20),
        name="solve",
    )(near, far, front_rhs, coupling, one, two)


def fold_kernel(kept_ref, came_ref, keep_ref, message_ref, send_ref, scales_ref):
    half, rows, _ = keep_ref.shape
    for i, value in enumerate(read_message(came_ref, rows, range(half, 2 * half))):
        send_ref[i] = kept_ref[half + i] + value
    write_message(message_ref, scales_ref, send_ref)
    for i, value in enumerate(read_message(came_ref, rows, range(half))):
        keep_ref[i] = kept_ref[i] + value


def fold(kept, came):
    count, rows, columns = kept.shape
    half = count // 2
    blocks = jax.ShapeDtypeStruct((half, rows, columns), jnp.float32)
    return pl.pallas_call(
        fold_kernel,
        out_shape=[blocks, message_shape(half, rows, columns)],
        in_specs=[VMEM] * 2,
        out_specs=[VMEM] * 2,
        scratch_shapes=[
            pltpu.VMEM(blocks.shape, jnp.float32),
            pltpu.VMEM((scale_rows(half), columns), jnp.float32),
        ],
        compiler_params=pltpu.CompilerParams(vmem_limit_bytes=24 * 2**20),
        name="fold",
    )(kept, came)


def last_kernel(kept_a, came_a, kept_b, came_b, out_ref):
    rows, columns = kept_a.shape[1:]
    for side, (kept, came) in enumerate(((kept_a, came_a), (kept_b, came_b))):
        out_ref[:, pl.ds(side * columns, columns)] = kept[0] + read_message(came, rows, [0])[0]


def last(kept_a, came_a, kept_b, came_b):
    _, rows, columns = kept_a.shape
    return pl.pallas_call(
        last_kernel,
        out_shape=jax.ShapeDtypeStruct((rows, 2 * columns), jnp.float32),
        in_specs=[VMEM] * 4,
        out_specs=VMEM,
        name="last",
    )(kept_a, came_a, kept_b, came_b)


def panel_dot(panel, rows):
    return lax.dot_general(
        panel, rows, (((0,), (0,)), ((), ())), preferred_element_type=jnp.float32
    )


def body(
    lower_panels,
    parent_solution,
    parent_rows,
    live_counts,
    front_rhs,
    coupling,
    inverse_one,
    inverse_two,
):
    groups = lax.axis_size("rows")
    shares = lax.axis_size("rhs")
    rows_dev = parent_rows.shape[0]
    slots = rows_dev // BLK // groups
    chunk_rows = slots * BLK
    bits = list(range(groups.bit_length() - 1))

    chunks = pack(lower_panels, parent_rows, live_counts, groups, slots)
    half = groups // 2
    mask_of = list(range(groups)) + [groups - 1]
    got, nears, fars = {0: chunks[0]}, {}, {}

    def after(value, *events):
        held = [store[key] for store, key in events]
        value, held = lax.optimization_barrier((value, held))
        for (store, key), now in zip(events, held):
            store[key] = now
        return value

    def move(at, *events):
        got[at] = swap(after(chunks[at], *events), "rows", mask_of[at])

    def cross(at, *events):
        own = after(got[at], *events)
        nears[at] = jnp.concatenate(
            [own] + [swap(own, "rhs", other) for other in range(2, shares, 2)], axis=1
        )

    runs = [[0], list(range(1, half)), [half, half + 1]] + [[at] for at in range(half + 2, groups + 1)]
    for at in range(half, groups + 1):
        move(at, *([(got, at - 2)] if at >= half + 2 else []))
    for at in range(1, half):
        move(at, *([(got, at - 9)] if at > 9 else []))
    starts = [0]
    for at in range(groups):
        starts.append(starts[at] + chunks[at].shape[0])
    def cross(own):
        return jnp.concatenate(
            [own] + [swap(own, "rhs", other) for other in range(2, shares, 2)], axis=1
        )
    near_total = far_total = 0.0
    picked = pick(parent_solution, [got[at] for at in range(groups)], slots)
    def add(i):
        rows = [picked[starts[at] : starts[at] + chunks[at].shape[0]] for at in runs[i]]
        rows = jnp.concatenate(rows, axis=0)
        return near_total + panel_dot(nears[i], rows), far_total + panel_dot(fars[i], rows)
    done = 0
    for r, run in enumerate(runs):
        if r == len(runs) - 1:
            while done < len(runs) - 1 - 2:
                near_total, far_total = add(done)
                done += 1
            got[groups], near_total, far_total = lax.optimization_barrier((got[groups], near_total, far_total))
        nears[r] = cross(jnp.concatenate([got[at] for at in run], axis=0))
        fars[r] = swap(nears[r], "rhs", 1)
    while done < len(runs):
        near_total, far_total = add(done)
        done += 1

    orders = (bits[1:] + bits[:1], bits)
    kept, sent = [None, None], [None, None]
    for side in range(2):
        kept[side], sent[side] = solve(
            side,
            orders[side],
            near_total,
            far_total,
            front_rhs,
            coupling,
            inverse_one,
            inverse_two,
            groups,
        )
    for step in range(len(bits)):
        came = [swap(sent[side], "rows", 1 << orders[side][step]) for side in range(2)]
        if step < len(bits) - 1:
            for side in range(2):
                kept[side], sent[side] = fold(kept[side], came[side])
    return last(kept[0], came[0], kept[1], came[1])


def solution(mesh):
    return jax.shard_map(
        body,
        mesh=mesh,
        in_specs=(
            P("rows", "rhs"),
            P("rows", "rhs"),
            P("rows"),
            P("rows"),
            P("rows", "rhs"),
            P(),
            P(),
            P(),
        ),
        out_specs=P("rows", "rhs"),
        check_vma=False,
    )
```

```python
import functools

import jax
import jax.numpy as jnp
from jax import lax
from jax.experimental import pallas as pl
from jax.experimental.pallas import tpu as pltpu
from jax.sharding import PartitionSpec as P

BLK = 128
LANES = 128
CODE_BITS = 14.96
WINDOW = 6
ANY = pl.BlockSpec(memory_space=pl.ANY)
VMEM = pl.BlockSpec(memory_space=pltpu.VMEM)
SMEM = pl.BlockSpec(memory_space=pltpu.SMEM)


def swap(array, axis, mask):
    size = lax.axis_size(axis)
    return lax.ppermute(array, axis, [(i, i ^ mask) for i in range(size)])


def pack_kernel(groups, slots, rows_ref, live_ref, lists_ref, panels_ref, *refs):
    chunks, place_ref, tile_ref = refs[:groups], refs[groups], refs[groups + 1]
    me = lax.axis_index("rows")
    rows_dev = rows_ref.shape[0]
    for place in range(groups):
        place_ref[lax.div(rows_ref[place * BLK], rows_dev) ^ me] = place
    live_blocks = lax.div(live_ref[0], BLK)
    tile_ref[...] = jnp.zeros_like(tile_ref)
    for mask in range(groups):
        start = (mask ^ me) * rows_dev
        for slot in range(slots):
            row = slot * groups + place_ref[mask]
            local = lists_ref[pl.ds(row, 1), :] - start
            tile_ref[pl.ds(2 * slot, 1), pl.ds(0, BLK)] = (local >> 8).astype(jnp.float32)
            tile_ref[pl.ds(2 * slot + 1, 1), pl.ds(0, BLK)] = (local & 255).astype(jnp.float32)
        chunk = chunks[mask]
        tile = tile_ref.shape[0]
        chunk[pl.ds(chunk.shape[0] - tile, tile), :] = tile_ref[...].astype(chunk.dtype)
        for slot in range(slots):
            block = slot * groups + place_ref[mask]
            into = (pl.ds(slot * BLK, BLK), slice(None))

            @pl.when(block < live_blocks)
            def _():
                chunk[into] = panels_ref[pl.ds(pl.multiple_of(block * BLK, BLK), BLK), :]

            @pl.when(block >= live_blocks)
            def _():
                chunk[into] = jnp.zeros((BLK, chunk.shape[1]), chunk.dtype)


def list_rows(slots):
    return -(-2 * slots // 16) * 16


def pack(lower_panels, parent_rows, live_counts, groups, slots):
    rows_dev, width = lower_panels.shape
    extra = list_rows(slots)
    chunk = jax.ShapeDtypeStruct((slots * BLK + extra, width), lower_panels.dtype)
    return pl.pallas_call(
        functools.partial(pack_kernel, groups, slots),
        out_shape=[chunk] * groups,
        in_specs=[SMEM, SMEM, VMEM, VMEM],
        out_specs=[VMEM] * groups,
        scratch_shapes=[
            pltpu.SMEM((groups,), jnp.int32),
            pltpu.VMEM((extra, width), jnp.float32),
        ],
        compiler_params=pltpu.CompilerParams(vmem_limit_bytes=24 * 2**20),
        name="pack",
    )(parent_rows, live_counts, parent_rows.reshape(rows_dev // BLK, BLK), lower_panels)


def pick_kernel(groups, slots, parent_ref, *refs):
    chunks, (out_ref, wide, stage, tiles_ref, lists_ref, rows_ref, sems) = refs[:groups], refs[groups:]
    extra = list_rows(slots)
    reads = []
    for mask, chunk in enumerate(chunks):
        from_ref = chunk.at[pl.ds(chunk.shape[0] - extra, extra), :]
        reads.append(pltpu.make_async_copy(from_ref, tiles_ref.at[mask], sems.at[mask]))
        reads[-1].start()
    for read in reads:
        read.wait()
    rows, columns = parent_ref.shape
    tiles = columns // LANES
    for mask in range(groups):
        for slot in range(slots):
            pair = tiles_ref[mask, :, pl.ds(0, BLK)].astype(jnp.float32)[2 * slot : 2 * slot + 2]
            local = pair[0:1] * 256.0 + pair[1:2]
            lists_ref[pl.ds(mask * slots + slot, 1), :] = local.astype(jnp.int32) * tiles
    move = pltpu.make_async_copy(lists_ref, rows_ref, sems.at[groups])
    move.start()
    step = min(rows, 256)

    @pl.loop(0, rows // step)
    def _(i):
        at = pl.multiple_of(i * step, step)
        for tile in range(tiles):
            wide[pl.ds(at * tiles + tile, step, stride=tiles), :] = parent_ref[
                pl.ds(at, step), pl.ds(tile * LANES, LANES)
            ].astype(jnp.float32)

    move.wait()
    nothing = jnp.zeros((extra, columns), out_ref.dtype)
    count = slots * BLK

    @pl.loop(0, groups)
    def _(mask):
        @pl.loop(0, slots)
        def _(slot):
            base = slot * (BLK * tiles)
            for i in range(BLK):
                row = pl.multiple_of(rows_ref[mask * slots + slot, i], tiles)
                into = pl.multiple_of(base + i * tiles, tiles)
                stage[pl.ds(into, tiles), :] = wide[pl.ds(row, tiles), :]

        into = pl.multiple_of(mask * (count + extra), 16)
        for tile in range(tiles):
            out_ref[pl.ds(into, count), pl.ds(tile * LANES, LANES)] = stage[
                pl.ds(tile, count, stride=tiles), :
            ].astype(out_ref.dtype)
        out_ref[pl.ds(pl.multiple_of(into + count, 16), extra), :] = nothing


def pick(parent, chunks, slots):
    groups = len(chunks)
    columns = parent.shape[1]
    tiles = columns // LANES
    extra = list_rows(slots)
    width = chunks[0].shape[1]
    return pl.pallas_call(
        functools.partial(pick_kernel, groups, slots),
        out_shape=jax.ShapeDtypeStruct((groups * (slots * BLK + extra), columns), parent.dtype),
        in_specs=[VMEM] + [ANY] * groups,
        out_specs=VMEM,
        scratch_shapes=[
            pltpu.VMEM((parent.shape[0] * tiles, LANES), jnp.float32),
            pltpu.VMEM((slots * BLK * tiles, LANES), jnp.float32),
            pltpu.VMEM((groups, extra, width), parent.dtype),
            pltpu.VMEM((groups * slots, BLK), jnp.int32),
            pltpu.SMEM((groups * slots, BLK), jnp.int32),
            pltpu.SemaphoreType.DMA((groups + 1,)),
        ],
        compiler_params=pltpu.CompilerParams(vmem_limit_bytes=48 * 2**20),
        name="pick",
    )(parent, *chunks)


def split(value):
    high = value.astype(jnp.bfloat16)
    return high, (value - high.astype(jnp.float32)).astype(jnp.bfloat16)


def dot3(left, right):
    dot = functools.partial(jnp.dot, preferred_element_type=jnp.float32)
    (lh, ll), (rh, rl) = left, right
    return dot(lh, rh) + (dot(lh, rl) + dot(ll, rh))


def encode(value):
    value = value * 0.25
    most = jnp.maximum(jnp.max(jnp.abs(value), axis=0, keepdims=True), 1e-30)
    exponent = jnp.floor(8.0 * jnp.log2(most)) + 1.0
    codes = jnp.round(value * jnp.exp2(CODE_BITS - 0.125 * exponent))
    return codes.astype(jnp.int32).astype(jnp.int16), exponent


def decode(codes, exponent):
    scale = jnp.exp2(0.125 * exponent - CODE_BITS)
    return codes.astype(jnp.int32).astype(jnp.float32) * scale * 4.0


def scale_rows(blocks):
    return -(-blocks // 16) * 16


def write_message(message_ref, scales_ref, blocks):
    count, rows, _ = blocks.shape
    scales_ref[...] = jnp.zeros_like(scales_ref)
    for i in range(count):
        codes, exponent = encode(blocks[i])
        message_ref[pl.ds(i * rows, rows), :] = codes
        scales_ref[pl.ds(i, 1), :] = exponent
    message_ref[pl.ds(count * rows, scales_ref.shape[0]), :] = (
        scales_ref[...].astype(jnp.int32).astype(jnp.int16)
    )


def read_message(message_ref, rows, wanted):
    count = message_ref.shape[0] // rows
    tail = message_ref[pl.ds(count * rows, message_ref.shape[0] - count * rows), :]
    exponents = tail.astype(jnp.int32).astype(jnp.float32)
    return [decode(message_ref[pl.ds(i * rows, rows), :], exponents[i : i + 1]) for i in wanted]


def message_shape(blocks, rows, columns):
    return jax.ShapeDtypeStruct((blocks * rows + scale_rows(blocks), columns), jnp.int16)


def solve_kernel(side, order, near_ref, far_ref, front_ref, coup_ref, one_ref, two_ref, *refs):
    keep_ref, message_ref, resid, send_ref, scales_ref = refs
    me = lax.axis_index("rows")
    share = lax.axis_index("rhs")
    pivot_share = front_ref.shape[0]
    pivots, columns = resid.shape
    panel = pivots // 2
    half_shares = lax.axis_size("rhs") // 2
    width = near_ref.shape[0] // half_shares
    groups = pivots // pivot_share
    cols = pl.ds(side * columns, columns)
    for odd, part_ref in ((0, near_ref), (1, far_ref)):
        for i in range(half_shares):
            at = pl.multiple_of((share ^ (2 * i + odd)) * width, width)
            resid[pl.ds(at, width), :] = -part_ref[pl.ds(i * width, width), cols]
    mine = pl.ds(pl.multiple_of(me * pivot_share, pivot_share), pivot_share)
    resid[mine, :] += front_ref[:, cols].astype(jnp.float32)
    second = dot3(split(two_ref[...]), split(resid[pl.ds(panel, panel), :]))
    reduced = resid[pl.ds(0, panel), :] - dot3(split(coup_ref[...]), split(second))
    first = dot3(split(one_ref[...]), split(reduced))
    for block in range(groups):
        source = first if block < groups // 2 else second
        at = (block % (groups // 2)) * pivot_share
        value = source[at : at + pivot_share, :]
        rel = block ^ me
        place = sum(
            ((rel >> bit) & 1) << (len(order) - 1 - i) for i, bit in enumerate(order) if i
        )
        sent = (rel >> order[0]) & 1

        @pl.when(sent == 0)
        def _():
            keep_ref[place] = value

        @pl.when(sent == 1)
        def _():
            send_ref[place] = value

    write_message(message_ref, scales_ref, send_ref)


def solve(side, order, near, far, front_rhs, coupling, one, two, groups):
    pivot_share, columns = front_rhs.shape
    pivots, columns, half = groups * pivot_share, columns // 2, groups // 2
    blocks = jax.ShapeDtypeStruct((half, pivot_share, columns), jnp.float32)
    return pl.pallas_call(
        functools.partial(solve_kernel, side, order),
        out_shape=[blocks, message_shape(half, pivot_share, columns)],
        in_specs=[VMEM] * 6,
        out_specs=[VMEM] * 2,
        scratch_shapes=[
            pltpu.VMEM((pivots, columns), jnp.float32),
            pltpu.VMEM(blocks.shape, jnp.float32),
            pltpu.VMEM((scale_rows(half), columns), jnp.float32),
        ],
        compiler_params=pltpu.CompilerParams(vmem_limit_bytes=48 * 2**20),
        name="solve",
    )(near, far, front_rhs, coupling, one, two)


def fold_kernel(kept_ref, came_ref, keep_ref, message_ref, send_ref, scales_ref):
    half, rows, _ = keep_ref.shape
    for i, value in enumerate(read_message(came_ref, rows, range(half, 2 * half))):
        send_ref[i] = kept_ref[half + i] + value
    write_message(message_ref, scales_ref, send_ref)
    for i, value in enumerate(read_message(came_ref, rows, range(half))):
        keep_ref[i] = kept_ref[i] + value


def fold(kept, came):
    count, rows, columns = kept.shape
    half = count // 2
    blocks = jax.ShapeDtypeStruct((half, rows, columns), jnp.float32)
    return pl.pallas_call(
        fold_kernel,
        out_shape=[blocks, message_shape(half, rows, columns)],
        in_specs=[VMEM] * 2,
        out_specs=[VMEM] * 2,
        scratch_shapes=[
            pltpu.VMEM(blocks.shape, jnp.float32),
            pltpu.VMEM((scale_rows(half), columns), jnp.float32),
        ],
        compiler_params=pltpu.CompilerParams(vmem_limit_bytes=24 * 2**20),
        name="fold",
    )(kept, came)


def last_kernel(kept_a, came_a, kept_b, came_b, out_ref):
    rows, columns = kept_a.shape[1:]
    for side, (kept, came) in enumerate(((kept_a, came_a), (kept_b, came_b))):
        out_ref[:, pl.ds(side * columns, columns)] = kept[0] + read_message(came, rows, [0])[0]


def last(kept_a, came_a, kept_b, came_b):
    _, rows, columns = kept_a.shape
    return pl.pallas_call(
        last_kernel,
        out_shape=jax.ShapeDtypeStruct((rows, 2 * columns), jnp.float32),
        in_specs=[VMEM] * 4,
        out_specs=VMEM,
        name="last",
    )(kept_a, came_a, kept_b, came_b)


def panel_dot(panel, rows):
    return lax.dot_general(
        panel, rows, (((0,), (0,)), ((), ())), preferred_element_type=jnp.float32
    )


def body(
    lower_panels,
    parent_solution,
    parent_rows,
    live_counts,
    front_rhs,
    coupling,
    inverse_one,
    inverse_two,
):
    groups = lax.axis_size("rows")
    shares = lax.axis_size("rhs")
    rows_dev = parent_rows.shape[0]
    slots = rows_dev // BLK // groups
    bits = list(range(groups.bit_length() - 1))
    half = groups // 2
    short, long = list(range(1, half)), list(range(half, groups))

    chunks = pack(lower_panels, parent_rows, live_counts, groups, slots)
    size = chunks[0].shape[0]

    runs = [[0], short[:-1], [short[-1], long[0]]] + [[mask] for mask in long[1:]]
    final = len(runs) - 1
    order = [("move", short[0]), ("move", long[0]), ("cross", 0)]
    order += [("move", mask) for mask in short[:0:-1]] + [("move", long[2]), ("cross", 1), ("cross", 2)]
    order += [("move", mask) for mask in long[3:]] + [("move", long[1])]
    loose = [("cross", run) for run in [final, *range(3, final)]] + [("pair", final)]
    order += loose
    store = {("move", 0): chunks[0]}
    picked, totals = {}, [0.0, 0.0]

    def pair(run):
        if ("pair", run) not in store:
            store["pair", run] = swap(store["cross", run], "rhs", 1)
        return store["pair", run]

    def add(run):
        for mask in runs[run]:
            if mask not in picked:
                masks = list(range(groups - 2)) if mask < groups - 2 else list(range(groups - 2, groups))
                rows = pick(parent_solution, [store["move", m] for m in masks], slots)
                for i, m in enumerate(masks):
                    picked[m] = rows[i * size : (i + 1) * size]
        rows = jnp.concatenate([picked[mask] for mask in runs[run]], axis=0)
        for side, panels in enumerate((store["cross", run], pair(run))):
            totals[side] = totals[side] + panel_dot(panels, rows)

    early = range(final - 1)
    for at, event in enumerate(order):
        kind, which = event
        if event == ("pair", final):
            for run in early:
                add(run)
        if kind == "move":
            value = chunks[which]
        elif kind == "cross":
            value = jnp.concatenate([store["move", mask] for mask in runs[which]], axis=0)
        else:
            value = store["cross", which]
        if at >= WINDOW and event not in loose:
            ahead = order[at - WINDOW]
            value, store[ahead] = lax.optimization_barrier((value, store[ahead]))
        if event == ("pair", final):
            value, *totals = lax.optimization_barrier((value, *totals))
        if kind == "move":
            store[event] = swap(value, "rows", which)
        elif kind == "cross":
            others = [swap(value, "rhs", other) for other in range(2, shares, 2)]
            store[event] = jnp.concatenate([value] + others, axis=1)
        else:
            store[event] = swap(value, "rhs", 1)
    for run in range(len(early), len(runs)):
        add(run)
    near_total, far_total = totals

    orders = (bits[1:] + bits[:1], bits)
    kept, sent = [None, None], [None, None]
    for side in range(2):
        kept[side], sent[side] = solve(
            side,
            orders[side],
            near_total,
            far_total,
            front_rhs,
            coupling,
            inverse_one,
            inverse_two,
            groups,
        )
    for step in range(len(bits)):
        came = [swap(sent[side], "rows", 1 << orders[side][step]) for side in range(2)]
        if step < len(bits) - 1:
            for side in range(2):
                kept[side], sent[side] = fold(kept[side], came[side])
    return last(kept[0], came[0], kept[1], came[1])


def solution(mesh):
    return jax.shard_map(
        body,
        mesh=mesh,
        in_specs=(
            P("rows", "rhs"),
            P("rows", "rhs"),
            P("rows"),
            P("rows"),
            P("rows", "rhs"),
            P(),
            P(),
            P(),
        ),
        out_specs=P("rows", "rhs"),
        check_vma=False,
    )
```

```python
import functools

import jax
import jax.numpy as jnp
from jax import lax
from jax.experimental import pallas as pl
from jax.experimental.pallas import tpu as pltpu
from jax.sharding import PartitionSpec as P

BLK = 128
LANES = 128
CODE_BITS = 14.96
WINDOW = 6
ANY = pl.BlockSpec(memory_space=pl.ANY)
VMEM = pl.BlockSpec(memory_space=pltpu.VMEM)
SMEM = pl.BlockSpec(memory_space=pltpu.SMEM)


def swap(array, axis, mask):
    size = lax.axis_size(axis)
    return lax.ppermute(array, axis, [(i, i ^ mask) for i in range(size)])


def pack_kernel(groups, slots, rows_ref, live_ref, lists_ref, panels_ref, *refs):
    chunks, place_ref, tile_ref = refs[:groups], refs[groups], refs[groups + 1]
    me = lax.axis_index("rows")
    rows_dev = rows_ref.shape[0]
    for place in range(groups):
        place_ref[lax.div(rows_ref[place * BLK], rows_dev) ^ me] = place
    live_blocks = lax.div(live_ref[0], BLK)
    tile_ref[...] = jnp.zeros_like(tile_ref)
    for mask in range(groups):
        start = (mask ^ me) * rows_dev
        for slot in range(slots):
            row = slot * groups + place_ref[mask]
            local = lists_ref[pl.ds(row, 1), :] - start
            tile_ref[pl.ds(2 * slot, 1), pl.ds(0, BLK)] = (local >> 8).astype(jnp.float32)
            tile_ref[pl.ds(2 * slot + 1, 1), pl.ds(0, BLK)] = (local & 255).astype(jnp.float32)
        chunk = chunks[mask]
        tile = tile_ref.shape[0]
        chunk[pl.ds(chunk.shape[0] - tile, tile), :] = tile_ref[...].astype(chunk.dtype)
        for slot in range(slots):
            block = slot * groups + place_ref[mask]
            into = (pl.ds(slot * BLK, BLK), slice(None))

            @pl.when(block < live_blocks)
            def _():
                chunk[into] = panels_ref[pl.ds(pl.multiple_of(block * BLK, BLK), BLK), :]

            @pl.when(block >= live_blocks)
            def _():
                chunk[into] = jnp.zeros((BLK, chunk.shape[1]), chunk.dtype)


def list_rows(slots):
    return -(-2 * slots // 16) * 16


def pack(lower_panels, parent_rows, live_counts, groups, slots):
    rows_dev, width = lower_panels.shape
    extra = list_rows(slots)
    chunk = jax.ShapeDtypeStruct((slots * BLK + extra, width), lower_panels.dtype)
    return pl.pallas_call(
        functools.partial(pack_kernel, groups, slots),
        out_shape=[chunk] * groups,
        in_specs=[SMEM, SMEM, VMEM, VMEM],
        out_specs=[VMEM] * groups,
        scratch_shapes=[
            pltpu.SMEM((groups,), jnp.int32),
            pltpu.VMEM((extra, width), jnp.float32),
        ],
        compiler_params=pltpu.CompilerParams(vmem_limit_bytes=24 * 2**20),
        name="pack",
    )(parent_rows, live_counts, parent_rows.reshape(rows_dev // BLK, BLK), lower_panels)


def pick_kernel(groups, slots, parent_ref, *refs):
    chunks, (out_ref, wide, stage, tiles_ref, lists_ref, rows_ref, sems) = refs[:groups], refs[groups:]
    extra = list_rows(slots)
    reads = []
    for mask, chunk in enumerate(chunks):
        from_ref = chunk.at[pl.ds(chunk.shape[0] - extra, extra), :]
        reads.append(pltpu.make_async_copy(from_ref, tiles_ref.at[mask], sems.at[mask]))
        reads[-1].start()
    for read in reads:
        read.wait()
    rows, columns = parent_ref.shape
    tiles = columns // LANES
    for mask in range(groups):
        for slot in range(slots):
            pair = tiles_ref[mask, :, pl.ds(0, BLK)].astype(jnp.float32)[2 * slot : 2 * slot + 2]
            local = pair[0:1] * 256.0 + pair[1:2]
            lists_ref[pl.ds(mask * slots + slot, 1), :] = local.astype(jnp.int32) * tiles
    move = pltpu.make_async_copy(lists_ref, rows_ref, sems.at[groups])
    move.start()
    step = min(rows, 256)

    @pl.loop(0, rows // step)
    def _(i):
        at = pl.multiple_of(i * step, step)
        for tile in range(tiles):
            wide[pl.ds(at * tiles + tile, step, stride=tiles), :] = parent_ref[
                pl.ds(at, step), pl.ds(tile * LANES, LANES)
            ].astype(jnp.float32)

    move.wait()
    nothing = jnp.zeros((extra, columns), out_ref.dtype)
    count = slots * BLK

    @pl.loop(0, groups)
    def _(mask):
        @pl.loop(0, slots)
        def _(slot):
            base = slot * (BLK * tiles)
            for i in range(BLK):
                row = pl.multiple_of(rows_ref[mask * slots + slot, i], tiles)
                into = pl.multiple_of(base + i * tiles, tiles)
                stage[pl.ds(into, tiles), :] = wide[pl.ds(row, tiles), :]

        into = pl.multiple_of(mask * (count + extra), 16)
        for tile in range(tiles):
            out_ref[pl.ds(into, count), pl.ds(tile * LANES, LANES)] = stage[
                pl.ds(tile, count, stride=tiles), :
            ].astype(out_ref.dtype)
        out_ref[pl.ds(pl.multiple_of(into + count, 16), extra), :] = nothing


def pick(parent, chunks, slots):
    groups = len(chunks)
    columns = parent.shape[1]
    tiles = columns // LANES
    extra = list_rows(slots)
    width = chunks[0].shape[1]
    return pl.pallas_call(
        functools.partial(pick_kernel, groups, slots),
        out_shape=jax.ShapeDtypeStruct((groups * (slots * BLK + extra), columns), parent.dtype),
        in_specs=[VMEM] + [ANY] * groups,
        out_specs=VMEM,
        scratch_shapes=[
            pltpu.VMEM((parent.shape[0] * tiles, LANES), jnp.float32),
            pltpu.VMEM((slots * BLK * tiles, LANES), jnp.float32),
            pltpu.VMEM((groups, extra, width), parent.dtype),
            pltpu.VMEM((groups * slots, BLK), jnp.int32),
            pltpu.SMEM((groups * slots, BLK), jnp.int32),
            pltpu.SemaphoreType.DMA((groups + 1,)),
        ],
        compiler_params=pltpu.CompilerParams(vmem_limit_bytes=48 * 2**20),
        name="pick",
    )(parent, *chunks)


def split(value):
    high = value.astype(jnp.bfloat16)
    return high, (value - high.astype(jnp.float32)).astype(jnp.bfloat16)


def dot3(left, right):
    dot = functools.partial(jnp.dot, preferred_element_type=jnp.float32)
    (lh, ll), (rh, rl) = left, right
    return dot(lh, rh) + (dot(lh, rl) + dot(ll, rh))


def triangle_dot(matrix, rows):
    half = matrix[0].shape[0] // 2
    upper = dot3([part[:half] for part in matrix], rows)
    lower = dot3([part[half:, half:] for part in matrix], [part[half:] for part in rows])
    return jnp.concatenate([upper, lower], axis=0)


def encode(value):
    value = value * 0.25
    most = jnp.maximum(jnp.max(jnp.abs(value), axis=0, keepdims=True), 1e-30)
    exponent = jnp.floor(8.0 * jnp.log2(most)) + 1.0
    codes = jnp.round(value * jnp.exp2(CODE_BITS - 0.125 * exponent))
    return codes.astype(jnp.int32).astype(jnp.int16), exponent


def decode(codes, exponent):
    scale = jnp.exp2(0.125 * exponent - CODE_BITS)
    return codes.astype(jnp.int32).astype(jnp.float32) * scale * 4.0


def scale_rows(blocks):
    return -(-blocks // 16) * 16


def write_message(message_ref, scales_ref, blocks):
    count, rows, _ = blocks.shape
    scales_ref[...] = jnp.zeros_like(scales_ref)
    for i in range(count):
        codes, exponent = encode(blocks[i])
        message_ref[pl.ds(i * rows, rows), :] = codes
        scales_ref[pl.ds(i, 1), :] = exponent
    message_ref[pl.ds(count * rows, scales_ref.shape[0]), :] = (
        scales_ref[...].astype(jnp.int32).astype(jnp.int16)
    )


def read_message(message_ref, rows, wanted):
    count = message_ref.shape[0] // rows
    tail = message_ref[pl.ds(count * rows, message_ref.shape[0] - count * rows), :]
    exponents = tail.astype(jnp.int32).astype(jnp.float32)
    return [decode(message_ref[pl.ds(i * rows, rows), :], exponents[i : i + 1]) for i in wanted]


def message_shape(blocks, rows, columns):
    return jax.ShapeDtypeStruct((blocks * rows + scale_rows(blocks), columns), jnp.int16)


def solve_kernel(side, order, near_ref, far_ref, front_ref, coup_ref, one_ref, two_ref, *refs):
    keep_ref, message_ref, resid, send_ref, scales_ref = refs
    me = lax.axis_index("rows")
    share = lax.axis_index("rhs")
    pivot_share = front_ref.shape[0]
    pivots, columns = resid.shape
    panel = pivots // 2
    half_shares = lax.axis_size("rhs") // 2
    width = near_ref.shape[0] // half_shares
    groups = pivots // pivot_share
    cols = pl.ds(side * columns, columns)
    for odd, part_ref in ((0, near_ref), (1, far_ref)):
        for i in range(half_shares):
            at = pl.multiple_of((share ^ (2 * i + odd)) * width, width)
            resid[pl.ds(at, width), :] = -part_ref[pl.ds(i * width, width), cols]
    mine = pl.ds(pl.multiple_of(me * pivot_share, pivot_share), pivot_share)
    resid[mine, :] += front_ref[:, cols].astype(jnp.float32)
    second = triangle_dot(split(two_ref[...]), split(resid[pl.ds(panel, panel), :]))
    reduced = resid[pl.ds(0, panel), :] - dot3(split(coup_ref[...]), split(second))
    first = triangle_dot(split(one_ref[...]), split(reduced))
    for block in range(groups):
        source = first if block < groups // 2 else second
        at = (block % (groups // 2)) * pivot_share
        value = source[at : at + pivot_share, :]
        rel = block ^ me
        place = sum(
            ((rel >> bit) & 1) << (len(order) - 1 - i) for i, bit in enumerate(order) if i
        )
        sent = (rel >> order[0]) & 1

        @pl.when(sent == 0)
        def _():
            keep_ref[place] = value

        @pl.when(sent == 1)
        def _():
            send_ref[place] = value

    write_message(message_ref, scales_ref, send_ref)


def solve(side, order, near, far, front_rhs, coupling, one, two, groups):
    pivot_share, columns = front_rhs.shape
    pivots, columns, half = groups * pivot_share, columns // 2, groups // 2
    blocks = jax.ShapeDtypeStruct((half, pivot_share, columns), jnp.float32)
    return pl.pallas_call(
        functools.partial(solve_kernel, side, order),
        out_shape=[blocks, message_shape(half, pivot_share, columns)],
        in_specs=[VMEM] * 6,
        out_specs=[VMEM] * 2,
        scratch_shapes=[
            pltpu.VMEM((pivots, columns), jnp.float32),
            pltpu.VMEM(blocks.shape, jnp.float32),
            pltpu.VMEM((scale_rows(half), columns), jnp.float32),
        ],
        compiler_params=pltpu.CompilerParams(vmem_limit_bytes=48 * 2**20),
        name="solve",
    )(near, far, front_rhs, coupling, one, two)


def fold_kernel(kept_ref, came_ref, keep_ref, message_ref, send_ref, scales_ref):
    half, rows, _ = keep_ref.shape
    for i, value in enumerate(read_message(came_ref, rows, range(half, 2 * half))):
        send_ref[i] = kept_ref[half + i] + value
    write_message(message_ref, scales_ref, send_ref)
    for i, value in enumerate(read_message(came_ref, rows, range(half))):
        keep_ref[i] = kept_ref[i] + value


def fold(kept, came):
    count, rows, columns = kept.shape
    half = count // 2
    blocks = jax.ShapeDtypeStruct((half, rows, columns), jnp.float32)
    return pl.pallas_call(
        fold_kernel,
        out_shape=[blocks, message_shape(half, rows, columns)],
        in_specs=[VMEM] * 2,
        out_specs=[VMEM] * 2,
        scratch_shapes=[
            pltpu.VMEM(blocks.shape, jnp.float32),
            pltpu.VMEM((scale_rows(half), columns), jnp.float32),
        ],
        compiler_params=pltpu.CompilerParams(vmem_limit_bytes=24 * 2**20),
        name="fold",
    )(kept, came)


def last_kernel(kept_a, came_a, kept_b, came_b, out_ref):
    rows, columns = kept_a.shape[1:]
    for side, (kept, came) in enumerate(((kept_a, came_a), (kept_b, came_b))):
        out_ref[:, pl.ds(side * columns, columns)] = kept[0] + read_message(came, rows, [0])[0]


def last(kept_a, came_a, kept_b, came_b):
    _, rows, columns = kept_a.shape
    return pl.pallas_call(
        last_kernel,
        out_shape=jax.ShapeDtypeStruct((rows, 2 * columns), jnp.float32),
        in_specs=[VMEM] * 4,
        out_specs=VMEM,
        name="last",
    )(kept_a, came_a, kept_b, came_b)


def panel_dot(panel, rows):
    return lax.dot_general(
        panel, rows, (((0,), (0,)), ((), ())), preferred_element_type=jnp.float32
    )


def body(
    lower_panels,
    parent_solution,
    parent_rows,
    live_counts,
    front_rhs,
    coupling,
    inverse_one,
    inverse_two,
):
    groups = lax.axis_size("rows")
    shares = lax.axis_size("rhs")
    rows_dev = parent_rows.shape[0]
    slots = rows_dev // BLK // groups
    bits = list(range(groups.bit_length() - 1))
    half = groups // 2
    short, long = list(range(1, half)), list(range(half, groups))

    chunks = pack(lower_panels, parent_rows, live_counts, groups, slots)
    size = chunks[0].shape[0]

    runs = [[0], short[:-1], [short[-1], long[0]]] + [[mask] for mask in long[1:]]
    final = len(runs) - 1
    order = [("move", short[0]), ("move", long[0]), ("cross", 0)]
    order += [("move", mask) for mask in short[:0:-1]] + [("move", long[2]), ("cross", 1), ("cross", 2)]
    order += [("move", mask) for mask in long[3:]] + [("move", long[1])]
    loose = [("cross", run) for run in [final, *range(3, final)]] + [("pair", final)]
    order += loose
    store = {("move", 0): chunks[0]}
    picked, totals = {}, [0.0, 0.0]

    def pair(run):
        if ("pair", run) not in store:
            store["pair", run] = swap(store["cross", run], "rhs", 1)
        return store["pair", run]

    def add(run):
        for mask in runs[run]:
            if mask not in picked:
                masks = list(range(groups - 2)) if mask < groups - 2 else list(range(groups - 2, groups))
                rows = pick(parent_solution, [store["move", m] for m in masks], slots)
                for i, m in enumerate(masks):
                    picked[m] = rows[i * size : (i + 1) * size]
        rows = jnp.concatenate([picked[mask] for mask in runs[run]], axis=0)
        for side, panels in enumerate((store["cross", run], pair(run))):
            totals[side] = totals[side] + panel_dot(panels, rows)

    early = range(final - 1)
    for at, event in enumerate(order):
        kind, which = event
        if event == ("pair", final):
            for run in early:
                add(run)
        if kind == "move":
            value = chunks[which]
        elif kind == "cross":
            value = jnp.concatenate([store["move", mask] for mask in runs[which]], axis=0)
        else:
            value = store["cross", which]
        if at >= WINDOW and event not in loose:
            ahead = order[at - WINDOW]
            value, store[ahead] = lax.optimization_barrier((value, store[ahead]))
        if event == ("pair", final):
            value, *totals = lax.optimization_barrier((value, *totals))
        if kind == "move":
            store[event] = swap(value, "rows", which)
        elif kind == "cross":
            others = [swap(value, "rhs", other) for other in range(2, shares, 2)]
            store[event] = jnp.concatenate([value] + others, axis=1)
        else:
            store[event] = swap(value, "rhs", 1)
    for run in range(len(early), len(runs)):
        add(run)
    near_total, far_total = totals

    orders = (bits[1:] + bits[:1], bits)
    kept, sent = [None, None], [None, None]
    for side in range(2):
        kept[side], sent[side] = solve(
            side,
            orders[side],
            near_total,
            far_total,
            front_rhs,
            coupling,
            inverse_one,
            inverse_two,
            groups,
        )
    for step in range(len(bits)):
        came = [swap(sent[side], "rows", 1 << orders[side][step]) for side in range(2)]
        if step < len(bits) - 1:
            for side in range(2):
                kept[side], sent[side] = fold(kept[side], came[side])
    return last(kept[0], came[0], kept[1], came[1])


def solution(mesh):
    return jax.shard_map(
        body,
        mesh=mesh,
        in_specs=(
            P("rows", "rhs"),
            P("rows", "rhs"),
            P("rows"),
            P("rows"),
            P("rows", "rhs"),
            P(),
            P(),
            P(),
        ),
        out_specs=P("rows", "rhs"),
        check_vma=False,
    )
```
